512 devices in a mesh: gossip: 16 (over x_lo, y, core), fsdp: 32 (over z, x_hi).
Axes of the slice: x: 4 (x_hi: 2, x_lo: 2; x = x_hi * 2 + x_lo), y: 4, z: 16, core: 2. Of those that a mesh axis runs over, the one named last changes fastest.
Arguments:
- activations: bfloat16 [16, 4096, 4608], P('gossip', 'fsdp'), may hold values from -6 to 6
- norm_gain: float32 [16, 4608], P('gossip'), may hold values from -0.5 to 1
- key_grad: bfloat16 [16, 4096, 1024], P('gossip', 'fsdp'), may hold values from -6 to 6
- numerator: float32 [16, 4608, 1024], P('gossip', 'fsdp'), may hold values from -6 to 6
- push_weight: float32 [16], P('gossip'), may hold values from 0.5 to 2
- step_count: int32 [1], replicated, may hold values from 0 to 999
Outputs:
- keys: bfloat16 [16, 4096, 1024], P('gossip', 'fsdp')
- input_grad: bfloat16 [16, 4096, 4608], P('gossip', 'fsdp')
- new_numerator: float32 [16, 4608, 1024], P('gossip', 'fsdp')
- new_weight: float32 [16], P('gossip')
The draws below stay inside these ranges and needn't reach their ends.
All inputs are finite; a program needn't handle non-finite values.
Results may differ from the reference program's by a relative error of at most 0.0085.
Values may be sent and summed in bfloat16 or wider, within the bound.
No kernel may reach another device: no remote copies, remote signals or barrier semaphores. Data moves between devices by JAX's collectives and lax.ppermute only.
A program may use at most 128 MiB of HBM per device.

```python
import math
import jax
import jax.numpy as jnp
from jax import lax

D = 4608
KV = 1024
TOKENS = 4096
REPLICAS = 16
N_GOSSIP = 16


def steps_of(stream_key, dims, shards, least, largest):
    loudness, own = 1.0, jax.random.fold_in(stream_key, 6)
    for axis_at, blocks in shards:
        draws = jnp.exp(jax.random.uniform(jax.random.fold_in(own, axis_at), (blocks,), jnp.float32, least / len(shards), largest / len(shards)))
        loudness = loudness * jnp.repeat(draws, dims[axis_at] // blocks).reshape([-1 if axis == axis_at else 1 for axis in range(len(dims))])
    return loudness


def scatter_about(rng, dims, scale, most, split=(), kind=jnp.bfloat16):
    drawn = scale * jax.random.normal(rng, dims, jnp.float32)
    if split:
        drawn = drawn * steps_of(rng, dims, split, -0.22, 0.18)
    return jnp.clip(drawn, -most, most).astype(kind)


def setup_inputs(seed: int = 0) -> dict:
    splits = jax.random.split(jax.random.key(seed), 7)
    activations = scatter_about(splits[0], (REPLICAS, TOKENS, D), 1.0, 6.0, ((0, 16), (1, 32)))
    norm_gain = jnp.clip(-0.5 + 1.5 * jax.random.uniform(splits[1], (REPLICAS, D), jnp.float32) ** steps_of(splits[1], (REPLICAS, D), ((0, 16),), -0.2, 0.2), -0.5, 1.0)
    key_grad = scatter_about(splits[2], (REPLICAS, TOKENS, KV), 1.0, 6.0, ((0, 16), (1, 32)))
    numerator = scatter_about(splits[3], (REPLICAS, D, KV), 1.0, 6.0, ((0, 16), (1, 32)), jnp.float32)
    push_weight = jnp.clip(jnp.exp(math.log(2.0) - 1.3862944 * jax.random.uniform(splits[4], (REPLICAS,), jnp.float32) ** steps_of(splits[4], (REPLICAS,), ((0, 16),), -0.2, 0.2)), 0.5, 2.0)
    step_count = jax.random.randint(splits[5], (1,), 0, 1000).astype(jnp.int32)
    return dict(activations=activations, norm_gain=norm_gain, key_grad=key_grad, numerator=numerator, push_weight=push_weight, step_count=step_count)


learn_rate = 0.01

def replica_pass(items):
    rows, gain_row, grad_keys, weight_mat = items
    values = rows.astype(jnp.float32)
    inv_rms = lax.rsqrt(lax.optimization_barrier(jnp.mean(values * values, axis=-1, keepdims=True)) + 1e-06)
    unit = values * inv_rms
    factor = 1.0 + gain_row.astype(jnp.float32)
    normed = (unit * factor).astype(jnp.bfloat16)
    keys = jnp.dot(normed, weight_mat, preferred_element_type=jnp.float32).astype(jnp.bfloat16)
    dnormed = jnp.dot(grad_keys, weight_mat.T, preferred_element_type=jnp.float32).astype(jnp.bfloat16)
    scaled = dnormed.astype(jnp.float32) * factor
    input_grad = (inv_rms * (scaled - unit * lax.optimization_barrier(jnp.mean(scaled * unit, axis=-1, keepdims=True)))).astype(jnp.bfloat16)
    grad = lax.dot_general(normed, grad_keys, (((0,), (0,)), ((), ())), preferred_element_type=jnp.float32)
    return (keys, input_grad, grad)

def reference(activations, norm_gain, key_grad, numerator, push_weight, step_count):
    levels = N_GOSSIP.bit_length() - 1
    param = (numerator / (push_weight[:, None, None] * math.sqrt(D))).astype(jnp.bfloat16)
    keys, input_grad, grad = lax.map(replica_pass, (activations, norm_gain, key_grad, param))
    chosen = jnp.remainder(step_count[0], levels).astype(jnp.int32)
    distance = jnp.left_shift(jnp.int32(1), chosen)
    source = jnp.remainder(jnp.arange(REPLICAS, dtype=jnp.int32) - distance, REPLICAS).astype(jnp.int32)
    new_numerator = 0.5 * (numerator - learn_rate * grad) + 0.5 * numerator[source]
    new_weight = 0.5 * (push_weight + push_weight[source])
    return (keys, input_grad, new_numerator, new_weight)
```

```python
from functools import partial
import math

import jax
import jax.numpy as jnp
from jax import lax
from jax.experimental import pallas as pl
from jax.experimental.pallas import tpu as pltpu
from jax.sharding import Mesh, PartitionSpec as P

learn_rate = 0.01
bf16, f32 = jnp.bfloat16, jnp.float32
LANES = 128
TN = (((0,), (0,)), ((), ()))
NT = (((1,), (1,)), ((), ()))


def sent(block, axis, distance):
    count = lax.axis_size(axis)
    return lax.ppermute(block, axis, [(i, (i + distance) % count) for i in range(count)])


def together(*arrays):
    return lax.optimization_barrier(arrays)


def lanes(b):
    return pl.ds(b * LANES, LANES)


def call(body, outs, scratch=(), flops=0, size=0):
    shapes = [jax.ShapeDtypeStruct(s, d) for s, d in outs]

    def run(*arrays):
        spaces = [pltpu.SMEM if a.size < 3 else pltpu.VMEM for a in arrays]
        return pl.pallas_call(
            body,
            out_shape=shapes,
            in_specs=[pl.BlockSpec(memory_space=space) for space in spaces],
            out_specs=[pl.BlockSpec(memory_space=pltpu.VMEM)] * len(outs),
            scratch_shapes=list(scratch),
            compiler_params=pltpu.CompilerParams(vmem_limit_bytes=32 * 2**20),
            cost_estimate=pl.CostEstimate(flops=flops, bytes_accessed=size, transcendentals=0),
        )(*arrays)

    return run


def block(rows, place):
    return pl.ds(place * rows, rows)


def owned(rows, owner):
    return pl.ds(pl.multiple_of(owner * rows, 16), rows)


def block(rows, place):
    return pl.ds(place * rows, rows)


def owned(rows, owner):
    return pl.ds(pl.multiple_of(owner * rows, 16), rows)


def normalise(rows, ring, at, push, act, gain, grads, numer, mine, send, inv, param, message, turned):
    param[...] = (numer[...] / (push[0] * math.sqrt(act.shape[1]))).astype(bf16)
    message[pl.ds(0, rows), :] = numer[...].astype(bf16)
    message[pl.ds(rows, 16), :] = jnp.full((16, numer.shape[1]), push[0], f32).astype(bf16)
    (tokens, width), z, h = act.shape, at[0], at[1]
    squares = jnp.zeros((tokens, LANES), f32)
    for b in range(width // LANES):
        x = act[:, lanes(b)].astype(f32)
        squares = squares + x * x
    scale = lax.rsqrt(jnp.sum(squares, axis=1, keepdims=True) / width + 1e-06)
    inv[...] = scale
    for b in range(width // LANES):
        unit = act[:, lanes(b)].astype(f32) * scale
        turned[lanes(b), :] = (unit * (1.0 + gain[:, lanes(b)])).T.astype(bf16)
    for place in range(ring):
        owner = lax.rem(z + place, ring)
        mine[block(rows, place), :] = turned[owned(rows, 2 * owner + h), :]
        send[block(rows, place), :] = turned[owned(rows, 2 * owner + 1 - h), :]
    for b in range(grads.shape[1] // LANES):
        send[pl.ds(width // 2 + b * tokens, tokens), :] = grads[:, lanes(b)]


def outer(rows, ring, at, mine, peer, grads, up, down, both):
    tokens, features = grads.shape
    both[pl.ds(0, tokens), :] = grads[...]
    for b in range(features // LANES):
        both[pl.ds(tokens, tokens), lanes(b)] = peer[pl.ds(mine.shape[0] + b * tokens, tokens), :]
    for place in range(ring):
        of = block(rows, place)
        normed = jnp.concatenate([mine[of, :], peer[of, :]], axis=1)
        product = jnp.dot(normed, both[...], preferred_element_type=f32).astype(bf16)
        if place < ring // 2:
            up[of, :] = product
        else:
            down[block(rows, place - ring // 2), :] = product


def project(rows, ring, at, mine, peer, both, *refs):
    blocks, (own, send, keys, total) = refs[:ring], refs[ring:]
    tokens, (half, features) = mine.shape[1], (mine.shape[0], both.shape[1])
    for place in range(ring):
        of = block(rows, place)
        weight = blocks[place][...]
        dnormed = lax.dot_general(weight, both[...], NT, preferred_element_type=f32).astype(bf16)
        own[of, :] = dnormed[:, :tokens]
        send[of, :] = dnormed[:, tokens:]
        normed = jnp.concatenate([mine[of, :], peer[of, :]], axis=1)
        product = lax.dot_general(normed, weight, TN, preferred_element_type=f32)
        if place:
            total[...] += product
        else:
            total[...] = product
    keys[...] = total[pl.ds(0, tokens), :]
    for b in range(features // LANES):
        send[pl.ds(half + b * tokens, tokens), :] = total[pl.ds(tokens, tokens), lanes(b)].astype(bf16)


def finish(rows, ring, at, own, got, act, gain, inv, part, keys, out, turned, scaled):
    (tokens, width), z, h = act.shape, at[0], at[1]
    for place in range(ring):
        owner = lax.rem(z + place, ring)
        turned[owned(rows, 2 * owner + h), :] = own[block(rows, place), :]
        turned[owned(rows, 2 * owner + 1 - h), :] = got[block(rows, place), :]
    scale = inv[...]
    products = jnp.zeros((tokens, LANES), f32)
    for b in range(width // LANES):
        value = turned[lanes(b), :].astype(f32).T * (1.0 + gain[:, lanes(b)])
        scaled[:, lanes(b)] = value
        products = products + value * (act[:, lanes(b)].astype(f32) * scale)
    mean = jnp.sum(products, axis=1, keepdims=True) / width
    for b in range(width // LANES):
        unit = act[:, lanes(b)].astype(f32) * scale
        out[:, lanes(b)] = (scale * (scaled[:, lanes(b)] - unit * mean)).astype(bf16)
    for b in range(part.shape[1] // LANES):
        received = got[pl.ds(width // 2 + b * tokens, tokens), :].astype(f32)
        keys[:, lanes(b)] = (part[:, lanes(b)] + received).astype(bf16)


def local(activations, norm_gain, key_grad, numerator, push_weight, step_count):
    rows_in, grad_keys, numer_rows = activations[0], key_grad[0], numerator[0]
    tokens, width = rows_in.shape
    ring = lax.axis_size("z")
    turns = ring // 2
    at = jnp.stack([lax.axis_index("z"), lax.axis_index("h")]).astype(jnp.int32)
    rows, features = numer_rows.shape
    half, tail = width // 2, features // LANES * tokens
    work = 2 * tokens * width * features
    arc = ((turns * rows, features), bf16)

    mine, send, inv_rms, param, message = call(
        partial(normalise, rows, ring),
        [((half, tokens), bf16), ((half + tail, tokens), bf16), ((tokens, 1), f32),
         ((rows, features), bf16), ((rows + 16, features), bf16)],
        [pltpu.VMEM((width, tokens), bf16)], 10 * tokens * width, 6 * tokens * width,
    )(at, push_weight, rows_in, norm_gain, grad_keys, numer_rows)
    peer = sent(send, "h", 1)
    held = {0: param}

    def gather(step):
        held[ring - step] = sent(held[(ring - step + 1) % ring], "z", 1)
        if step < turns:
            held[step] = sent(held[step - 1], "z", -1)

    def newest(step):
        return [(ring - step) % ring] + ([step] if 0 < step < turns else [])

    def after_gather(step, *arrays):
        places = newest(step)
        *blocks, = together(*[held[p] for p in places], *arrays)
        held.update(zip(places, blocks))
        return blocks[len(places):]

    gather(1)
    peer, = after_gather(1, peer)
    part_up, part_down, both = call(
        partial(outer, rows, ring), [arc, arc, ((2 * tokens, features), bf16)], (), work, 2 * half * features,
    )(at, mine, peer, grad_keys)

    def part(place):
        array, i = (part_up, place) if place >= 0 else (part_down, place + turns)
        return lax.slice_in_dim(array, i * rows, (i + 1) * rows)

    up, down = part(turns - 1), part(-turns)

    def scatter(step, up, down):
        down = sent(down, "z", -1)
        if step < turns:
            up, down = sent(up, "z", 1), down + part(step - turns)
            up = up + part(turns - 1 - step) if step < turns - 1 else up
        return up, down

    lag = 1
    for step in range(lag + 1, turns + 1):
        gather(step)
        up, down = after_gather(step - 1, up, down)
        up, down = scatter(step - lag, up, down)
        if step > lag + 1:
            after_gather(step, *sums)
        sums = up, down
    own, send_back, part_keys = call(
        partial(project, rows, ring),
        [((half, tokens), bf16), ((half + tail, tokens), bf16), ((tokens, features), f32)],
        [pltpu.VMEM((2 * tokens, features), f32)], 2 * work, 2 * half * features,
    )(at, mine, peer, both, *(held[place] for place in range(ring)))
    send_back, message = together(send_back, message)
    back = sent(send_back, "h", 1)
    levels = lax.axis_size("gossip").bit_length() - 1
    got = lax.switch(
        lax.rem(step_count[0], levels), [partial(sent, axis="gossip", distance=2**level) for level in range(levels)], message
    )
    for step in range(turns - lag + 1, turns + 1):
        up, down = scatter(step, up, down)
    keys, input_grad = call(
        partial(finish, rows, ring),
        [((tokens, features), bf16), ((tokens, width), bf16)],
        [pltpu.VMEM((width, tokens), bf16), pltpu.VMEM((tokens, width), f32)], 10 * tokens * width, 8 * tokens * width,
    )(at, own, back, rows_in, norm_gain, inv_rms, part_keys)

    grad_rows = part(0).astype(f32) + up.astype(f32) + down.astype(f32)
    peer_numer, peer_weight = got[:rows].astype(f32), got[rows, :1].astype(f32)
    new_numerator = 0.5 * (numer_rows - learn_rate * grad_rows) + 0.5 * peer_numer
    new_weight = 0.5 * (push_weight + peer_weight)
    return (keys[None], input_grad[None], new_numerator[None], new_weight)


def solution(mesh):
    replicas, members = mesh.devices.shape
    split = Mesh(mesh.devices.reshape(replicas, members // 2, 2), ("gossip", "z", "h"))
    both = ("z", "h")
    return jax.shard_map(
        local,
        mesh=split,
        in_specs=(
            P("gossip", both, None),
            P("gossip", None),
            P("gossip", both, None),
            P("gossip", both, None),
            P("gossip"),
            P(),
        ),
        out_specs=(
            P("gossip", both, None),
            P("gossip", both, None),
            P("gossip", both, None),
            P("gossip"),
        ),
        check_vma=False,
    )
```

```python
from functools import partial
import math

import jax
import jax.numpy as jnp
from jax import lax
from jax.experimental import pallas as pl
from jax.experimental.pallas import tpu as pltpu
from jax.sharding import Mesh, PartitionSpec as P

learn_rate = 0.01
bf16, f32 = jnp.bfloat16, jnp.float32
LANES = 128
TN = (((0,), (0,)), ((), ()))
NT = (((1,), (1,)), ((), ()))


def sent(block, axis, distance):
    count = lax.axis_size(axis)
    return lax.ppermute(block, axis, [(i, (i + distance) % count) for i in range(count)])


def together(*arrays):
    return lax.optimization_barrier(arrays)


def lanes(b):
    return pl.ds(b * LANES, LANES)


def call(body, outs, scratch=(), flops=0, size=0):
    shapes = [jax.ShapeDtypeStruct(s, d) for s, d in outs]

    def run(*arrays):
        spaces = [pltpu.SMEM if a.size < 3 else pltpu.VMEM for a in arrays]
        return pl.pallas_call(
            body,
            out_shape=shapes,
            in_specs=[pl.BlockSpec(memory_space=space) for space in spaces],
            out_specs=[pl.BlockSpec(memory_space=pltpu.VMEM)] * len(outs),
            scratch_shapes=list(scratch),
            compiler_params=pltpu.CompilerParams(vmem_limit_bytes=32 * 2**20),
            cost_estimate=pl.CostEstimate(flops=flops, bytes_accessed=size, transcendentals=0),
        )(*arrays)

    return run


def block(rows, place):
    return pl.ds(place * rows, rows)


def owned(rows, owner):
    return pl.ds(pl.multiple_of(owner * rows, 16), rows)


def block(rows, place):
    return pl.ds(place * rows, rows)


def owned(rows, owner):
    return pl.ds(pl.multiple_of(owner * rows, 16), rows)


def normalise(rows, ring, at, push, act, gain, grads, numer, mine, send, inv, param, message, turned):
    param[...] = (numer[...] / (push[0] * math.sqrt(act.shape[1]))).astype(bf16)
    message[pl.ds(0, rows), :] = numer[...].astype(bf16)
    message[pl.ds(rows, 16), :] = jnp.full((16, numer.shape[1]), push[0], f32).astype(bf16)
    (tokens, width), z, h = act.shape, at[0], at[1]
    squares = jnp.zeros((tokens, LANES), f32)
    for b in range(width // LANES):
        x = act[:, lanes(b)].astype(f32)
        squares = squares + x * x
    scale = lax.rsqrt(jnp.sum(squares, axis=1, keepdims=True) / width + 1e-06)
    inv[...] = scale
    for b in range(width // LANES):
        unit = act[:, lanes(b)].astype(f32) * scale
        turned[lanes(b), :] = (unit * (1.0 + gain[:, lanes(b)])).T.astype(bf16)
    for place in range(ring):
        owner = lax.rem(z + place, ring)
        mine[block(rows, place), :] = turned[owned(rows, 2 * owner + h), :]
        send[block(rows, place), :] = turned[owned(rows, 2 * owner + 1 - h), :]
    for b in range(grads.shape[1] // LANES):
        send[pl.ds(width // 2 + b * tokens, tokens), :] = grads[:, lanes(b)]


def outer(rows, ring, at, mine, peer, grads, up, down, both):
    tokens, features = grads.shape
    both[pl.ds(0, tokens), :] = grads[...]
    for b in range(features // LANES):
        both[pl.ds(tokens, tokens), lanes(b)] = peer[pl.ds(mine.shape[0] + b * tokens, tokens), :]
    for place in range(ring):
        of = block(rows, place)
        normed = jnp.concatenate([mine[of, :], peer[of, :]], axis=1)
        product = jnp.dot(normed, both[...], preferred_element_type=f32).astype(bf16)
        if place < ring // 2:
            up[of, :] = product
        else:
            down[block(rows, place - ring // 2), :] = product


def project(rows, ring, at, mine, peer, both, *refs):
    blocks, (own, send, keys, total) = refs[:ring], refs[ring:]
    tokens, (half, features) = mine.shape[1], (mine.shape[0], both.shape[1])
    for place in range(ring):
        of = block(rows, place)
        weight = blocks[place][...]
        dnormed = lax.dot_general(weight, both[...], NT, preferred_element_type=f32).astype(bf16)
        own[of, :] = dnormed[:, :tokens]
        send[of, :] = dnormed[:, tokens:]
        normed = jnp.concatenate([mine[of, :], peer[of, :]], axis=1)
        product = lax.dot_general(normed, weight, TN, preferred_element_type=f32)
        if place:
            total[...] += product
        else:
            total[...] = product
    keys[...] = total[pl.ds(0, tokens), :]
    for b in range(features // LANES):
        send[pl.ds(half + b * tokens, tokens), :] = total[pl.ds(tokens, tokens), lanes(b)].astype(bf16)


def finish(rows, ring, at, own, got, act, gain, inv, part, keys, out, turned, scaled):
    (tokens, width), z, h = act.shape, at[0], at[1]
    for place in range(ring):
        owner = lax.rem(z + place, ring)
        turned[owned(rows, 2 * owner + h), :] = own[block(rows, place), :]
        turned[owned(rows, 2 * owner + 1 - h), :] = got[block(rows, place), :]
    scale = inv[...]
    products = jnp.zeros((tokens, LANES), f32)
    for b in range(width // LANES):
        value = turned[lanes(b), :].astype(f32).T * (1.0 + gain[:, lanes(b)])
        scaled[:, lanes(b)] = value
        products = products + value * (act[:, lanes(b)].astype(f32) * scale)
    mean = jnp.sum(products, axis=1, keepdims=True) / width
    for b in range(width // LANES):
        unit = act[:, lanes(b)].astype(f32) * scale
        out[:, lanes(b)] = (scale * (scaled[:, lanes(b)] - unit * mean)).astype(bf16)
    for b in range(part.shape[1] // LANES):
        received = got[pl.ds(width // 2 + b * tokens, tokens), :].astype(f32)
        keys[:, lanes(b)] = (part[:, lanes(b)] + received).astype(bf16)


def local(activations, norm_gain, key_grad, numerator, push_weight, step_count):
    rows_in, grad_keys, numer_rows = activations[0], key_grad[0], numerator[0]
    tokens, width = rows_in.shape
    ring = lax.axis_size("z")
    turns = ring // 2
    at = jnp.stack([lax.axis_index("z"), lax.axis_index("h")]).astype(jnp.int32)
    rows, features = numer_rows.shape
    half, tail = width // 2, features // LANES * tokens
    work = 2 * tokens * width * features
    arc = ((turns * rows, features), bf16)

    mine, send, inv_rms, param, message = call(
        partial(normalise, rows, ring),
        [((half, tokens), bf16), ((half + tail, tokens), bf16), ((tokens, 1), f32),
         ((rows, features), bf16), ((rows + 16, features), bf16)],
        [pltpu.VMEM((width, tokens), bf16)], 10 * tokens * width, 6 * tokens * width,
    )(at, push_weight, rows_in, norm_gain, grad_keys, numer_rows)
    peer = sent(send, "h", 1)
    held = {0: param}

    def gather(step):
        held[ring - step] = sent(held[(ring - step + 1) % ring], "z", 1)
        if step < turns:
            held[step] = sent(held[step - 1], "z", -1)

    def newest(step):
        return [(ring - step) % ring] + ([step] if 0 < step < turns else [])

    def after_gather(step, *arrays):
        places = newest(step)
        *blocks, = together(*[held[p] for p in places], *arrays)
        held.update(zip(places, blocks))
        return blocks[len(places):]

    gather(1)
    levels = lax.axis_size("gossip").bit_length() - 1
    got = lax.switch(
        lax.rem(step_count[0], levels), [partial(sent, axis="gossip", distance=2**level) for level in range(levels)], message
    )
    peer, got = after_gather(1, peer, got)
    part_up, part_down, both = call(
        partial(outer, rows, ring), [arc, arc, ((2 * tokens, features), bf16)], (), work, 2 * half * features,
    )(at, mine, peer, grad_keys)

    def part(place):
        array, i = (part_up, place) if place >= 0 else (part_down, place + turns)
        return lax.slice_in_dim(array, i * rows, (i + 1) * rows)

    up, down = part(turns - 1), part(-turns)

    def scatter(step, up, down):
        down = sent(down, "z", -1)
        if step < turns:
            up, down = sent(up, "z", 1), down + part(step - turns)
            up = up + part(turns - 1 - step) if step < turns - 1 else up
        return up, down

    lag = 1
    for step in range(lag + 1, turns + 1):
        gather(step)
        up, down = after_gather(step - 1, up, down)
        up, down = scatter(step - lag, up, down)
        if step > lag + 1:
            after_gather(step, *sums)
        sums = up, down
    own, send_back, part_keys = call(
        partial(project, rows, ring),
        [((half, tokens), bf16), ((half + tail, tokens), bf16), ((tokens, features), f32)],
        [pltpu.VMEM((2 * tokens, features), f32)], 2 * work, 2 * half * features,
    )(at, mine, peer, both, *(held[place] for place in range(ring)))
    back = sent(send_back, "h", 1)
    for step in range(turns - lag + 1, turns + 1):
        up, down = scatter(step, up, down)
    keys, input_grad = call(
        partial(finish, rows, ring),
        [((tokens, features), bf16), ((tokens, width), bf16)],
        [pltpu.VMEM((width, tokens), bf16), pltpu.VMEM((tokens, width), f32)], 10 * tokens * width, 8 * tokens * width,
    )(at, own, back, rows_in, norm_gain, inv_rms, part_keys)

    grad_rows = part(0).astype(f32) + up.astype(f32) + down.astype(f32)
    peer_numer, peer_weight = got[:rows].astype(f32), got[rows, :1].astype(f32)
    new_numerator = 0.5 * (numer_rows - learn_rate * grad_rows) + 0.5 * peer_numer
    new_weight = 0.5 * (push_weight + peer_weight)
    return (keys[None], input_grad[None], new_numerator[None], new_weight)


def solution(mesh):
    replicas, members = mesh.devices.shape
    split = Mesh(mesh.devices.reshape(replicas, members // 2, 2), ("gossip", "z", "h"))
    both = ("z", "h")
    return jax.shard_map(
        local,
        mesh=split,
        in_specs=(
            P("gossip", both, None),
            P("gossip", None),
            P("gossip", both, None),
            P("gossip", both, None),
            P("gossip"),
            P(),
        ),
        out_specs=(
            P("gossip", both, None),
            P("gossip", both, None),
            P("gossip", both, None),
            P("gossip"),
        ),
        check_vma=False,
    )
```

```python
from functools import partial
import math

import jax
import jax.numpy as jnp
from jax import lax
from jax.experimental import pallas as pl
from jax.experimental.pallas import tpu as pltpu
from jax.sharding import Mesh, PartitionSpec as P

learn_rate = 0.01
bf16, f32 = jnp.bfloat16, jnp.float32
LANES = 128
TN = (((0,), (0,)), ((), ()))
NT = (((1,), (1,)), ((), ()))


def sent(block, axis, distance):
    count = lax.axis_size(axis)
    return lax.ppermute(block, axis, [(i, (i + distance) % count) for i in range(count)])


def together(*arrays):
    return lax.optimization_barrier(arrays)


def lanes(b):
    return pl.ds(b * LANES, LANES)


def call(body, outs, scratch=(), flops=0, size=0):
    shapes = [jax.ShapeDtypeStruct(s, d) for s, d in outs]

    def run(*arrays):
        spaces = [pltpu.SMEM if a.size < 3 else pltpu.VMEM for a in arrays]
        return pl.pallas_call(
            body,
            out_shape=shapes,
            in_specs=[pl.BlockSpec(memory_space=space) for space in spaces],
            out_specs=[pl.BlockSpec(memory_space=pltpu.VMEM)] * len(outs),
            scratch_shapes=list(scratch),
            compiler_params=pltpu.CompilerParams(vmem_limit_bytes=32 * 2**20),
            cost_estimate=pl.CostEstimate(flops=flops, bytes_accessed=size, transcendentals=0),
        )(*arrays)

    return run


def block(rows, place):
    return pl.ds(place * rows, rows)


def owned(rows, owner):
    return pl.ds(pl.multiple_of(owner * rows, 16), rows)


def block(rows, place):
    return pl.ds(place * rows, rows)


def owned(rows, owner):
    return pl.ds(pl.multiple_of(owner * rows, 16), rows)


def normalise(rows, ring, at, push, act, gain, grads, numer, mine, send, inv, param, message, turned):
    param[...] = (numer[...] / (push[0] * math.sqrt(act.shape[1]))).astype(bf16)
    message[pl.ds(0, rows), :] = numer[...].astype(bf16)
    message[pl.ds(rows, 16), :] = jnp.full((16, numer.shape[1]), push[0], f32).astype(bf16)
    (tokens, width), z, h = act.shape, at[0], at[1]
    squares = jnp.zeros((tokens, LANES), f32)
    for b in range(width // LANES):
        x = act[:, lanes(b)].astype(f32)
        squares = squares + x * x
    scale = lax.rsqrt(jnp.sum(squares, axis=1, keepdims=True) / width + 1e-06)
    inv[...] = scale
    for b in range(width // LANES):
        unit = act[:, lanes(b)].astype(f32) * scale
        turned[lanes(b), :] = (unit * (1.0 + gain[:, lanes(b)])).T.astype(bf16)
    for place in range(ring):
        owner = lax.rem(z + place, ring)
        mine[block(rows, place), :] = turned[owned(rows, 2 * owner + h), :]
        send[block(rows, place), :] = turned[owned(rows, 2 * owner + 1 - h), :]
    for b in range(grads.shape[1] // LANES):
        send[pl.ds(width // 2 + b * tokens, tokens), :] = grads[:, lanes(b)]


def product_at(rows, place, mine, peer, both):
    of = block(rows, place)
    normed = jnp.concatenate([mine[of, :], peer[of, :]], axis=1)
    return jnp.dot(normed, both[...], preferred_element_type=f32).astype(bf16)


def outer_far(rows, ring, at, mine, peer, grads, up, down, both):
    tokens, features = grads.shape
    both[pl.ds(0, tokens), :] = grads[...]
    for b in range(features // LANES):
        both[pl.ds(tokens, tokens), lanes(b)] = peer[pl.ds(mine.shape[0] + b * tokens, tokens), :]
    up[...] = product_at(rows, ring // 2 - 1, mine, peer, both)
    down[...] = product_at(rows, ring // 2, mine, peer, both)


def outer(rows, ring, at, mine, peer, both, up, down):
    for i in range(ring // 2 - 1):
        up[block(rows, i), :] = product_at(rows, i, mine, peer, both)
        down[block(rows, i), :] = product_at(rows, ring // 2 + 1 + i, mine, peer, both)


def project(rows, ring, at, mine, peer, both, *refs):
    blocks, (own, send, keys, total) = refs[:ring], refs[ring:]
    tokens, (half, features) = mine.shape[1], (mine.shape[0], both.shape[1])
    for place in range(ring):
        of = block(rows, place)
        weight = blocks[place][...]
        dnormed = lax.dot_general(weight, both[...], NT, preferred_element_type=f32).astype(bf16)
        own[of, :] = dnormed[:, :tokens]
        send[of, :] = dnormed[:, tokens:]
        normed = jnp.concatenate([mine[of, :], peer[of, :]], axis=1)
        product = lax.dot_general(normed, weight, TN, preferred_element_type=f32)
        if place:
            total[...] += product
        else:
            total[...] = product
    keys[...] = total[pl.ds(0, tokens), :]
    for b in range(features // LANES):
        send[pl.ds(half + b * tokens, tokens), :] = total[pl.ds(tokens, tokens), lanes(b)].astype(bf16)


def finish(rows, ring, at, own, got, act, gain, inv, part, keys, out, turned, scaled):
    (tokens, width), z, h = act.shape, at[0], at[1]
    for place in range(ring):
        owner = lax.rem(z + place, ring)
        turned[owned(rows, 2 * owner + h), :] = own[block(rows, place), :]
        turned[owned(rows, 2 * owner + 1 - h), :] = got[block(rows, place), :]
    scale = inv[...]
    products = jnp.zeros((tokens, LANES), f32)
    for b in range(width // LANES):
        value = turned[lanes(b), :].astype(f32).T * (1.0 + gain[:, lanes(b)])
        scaled[:, lanes(b)] = value
        products = products + value * (act[:, lanes(b)].astype(f32) * scale)
    mean = jnp.sum(products, axis=1, keepdims=True) / width
    for b in range(width // LANES):
        unit = act[:, lanes(b)].astype(f32) * scale
        out[:, lanes(b)] = (scale * (scaled[:, lanes(b)] - unit * mean)).astype(bf16)
    for b in range(part.shape[1] // LANES):
        received = got[pl.ds(width // 2 + b * tokens, tokens), :].astype(f32)
        keys[:, lanes(b)] = (part[:, lanes(b)] + received).astype(bf16)


def local(activations, norm_gain, key_grad, numerator, push_weight, step_count):
    rows_in, grad_keys, numer_rows = activations[0], key_grad[0], numerator[0]
    tokens, width = rows_in.shape
    ring = lax.axis_size("z")
    turns = ring // 2
    at = jnp.stack([lax.axis_index("z"), lax.axis_index("h")]).astype(jnp.int32)
    rows, features = numer_rows.shape
    half, tail = width // 2, features // LANES * tokens
    work = 2 * tokens * width * features
    arc = (((turns - 1) * rows, features), bf16)

    mine, send, inv_rms, param, message = call(
        partial(normalise, rows, ring),
        [((half, tokens), bf16), ((half + tail, tokens), bf16), ((tokens, 1), f32),
         ((rows, features), bf16), ((rows + 16, features), bf16)],
        [pltpu.VMEM((width, tokens), bf16)], 10 * tokens * width, 6 * tokens * width,
    )(at, push_weight, rows_in, norm_gain, grad_keys, numer_rows)
    peer = sent(send, "h", 1)
    held = {0: param}

    def gather(step):
        held[ring - step] = sent(held[(ring - step + 1) % ring], "z", 1)
        if step < turns:
            held[step] = sent(held[step - 1], "z", -1)

    def newest(step):
        return [(ring - step) % ring] + ([step] if 0 < step < turns else [])

    def after_gather(step, *arrays):
        places = newest(step)
        *blocks, = together(*[held[p] for p in places], *arrays)
        held.update(zip(places, blocks))
        return blocks[len(places):]

    gather(1)
    levels = lax.axis_size("gossip").bit_length() - 1
    got = lax.switch(
        lax.rem(step_count[0], levels), [partial(sent, axis="gossip", distance=2**level) for level in range(levels)], message
    )
    peer, got = after_gather(1, peer, got)
    up, down, both = call(
        partial(outer_far, rows, ring),
        [((rows, features), bf16), ((rows, features), bf16), ((2 * tokens, features), bf16)],
        (), work // turns, half * features // 4,
    )(at, mine, peer, grad_keys)
    part_up, part_down = call(
        partial(outer, rows, ring), [arc, arc], (), work, 2 * half * features,
    )(at, mine, peer, both)

    def part(place):
        array, i = (part_up, place) if place >= 0 else (part_down, place + turns - 1)
        return lax.slice_in_dim(array, i * rows, (i + 1) * rows)

    def scatter(step, up, down):
        down = sent(down, "z", -1)
        if step < turns:
            up, down = sent(up, "z", 1), down + part(step - turns)
            up = up + part(turns - 1 - step) if step < turns - 1 else up
        return up, down

    lag = 1
    for step in range(lag + 1, turns + 1):
        gather(step)
        up, down = after_gather(step - 1, up, down)
        up, down = scatter(step - lag, up, down)
        if step > lag + 1:
            after_gather(step, *sums)
        sums = up, down
    own, send_back, part_keys = call(
        partial(project, rows, ring),
        [((half, tokens), bf16), ((half + tail, tokens), bf16), ((tokens, features), f32)],
        [pltpu.VMEM((2 * tokens, features), f32)], 2 * work, 2 * half * features,
    )(at, mine, peer, both, *(held[place] for place in range(ring)))
    back = sent(send_back, "h", 1)
    for step in range(turns - lag + 1, turns + 1):
        up, down = scatter(step, up, down)
    keys, input_grad = call(
        partial(finish, rows, ring),
        [((tokens, features), bf16), ((tokens, width), bf16)],
        [pltpu.VMEM((width, tokens), bf16), pltpu.VMEM((tokens, width), f32)], 10 * tokens * width, 8 * tokens * width,
    )(at, own, back, rows_in, norm_gain, inv_rms, part_keys)

    grad_rows = part(0).astype(f32) + up.astype(f32) + down.astype(f32)
    peer_numer, peer_weight = got[:rows].astype(f32), got[rows, :1].astype(f32)
    new_numerator = 0.5 * (numer_rows - learn_rate * grad_rows) + 0.5 * peer_numer
    new_weight = 0.5 * (push_weight + peer_weight)
    return (keys[None], input_grad[None], new_numerator[None], new_weight)


def solution(mesh):
    replicas, members = mesh.devices.shape
    split = Mesh(mesh.devices.reshape(replicas, members // 2, 2), ("gossip", "z", "h"))
    both = ("z", "h")
    return jax.shard_map(
        local,
        mesh=split,
        in_specs=(
            P("gossip", both, None),
            P("gossip", None),
            P("gossip", both, None),
            P("gossip", both, None),
            P("gossip"),
            P(),
        ),
        out_specs=(
            P("gossip", both, None),
            P("gossip", both, None),
            P("gossip", both, None),
            P("gossip"),
        ),
        check_vma=False,
    )
```
